256 devices in a mesh: dp: 16 (over z, core), comp: 16 (over y, x).
Axes of the slice: x: 4, y: 4, z: 8, core: 2. Of those that a mesh axis runs over, the one named last changes fastest.
Arguments:
- points: bfloat16 [524288, 768], P(('dp', 'comp')), may hold values from -6 to 6
- candidates: int32 [4096, 4], P(('dp', 'comp')), may hold values from 0 to 511, as said below
- means: bfloat16 [65536, 768], P(('dp', 'comp')), may hold values from -0.59765625 to 0.59765625
- inv_var: bfloat16 [65536, 768], P(('dp', 'comp')), may hold values from 0.5 to 1.5
- log_weight: bfloat16 [65536], P(('dp', 'comp')), may hold values from -12 to -9
Outputs:
- counts: float32 [65536], P(('dp', 'comp'))
- first_moment: float32 [65536, 768], P(('dp', 'comp'))
- second_moment: float32 [65536, 768], P(('dp', 'comp'))
- loglik: float32 [524288], P(('dp', 'comp'))
The draws below stay inside these ranges and needn't reach their ends.
Inputs may be any that keep to these rules, and one draw needn't show every extreme that they name: `candidates`: each row block names 4 different component blocks; all blocks b named by the row blocks of device index i along dp+comp satisfy (b // 2) % 16 == i % 16, that is, one owner group serves each device's rows.
All inputs are finite; a program needn't handle non-finite values.
Results may differ from the reference program's by a relative error of at most 0.028.
Values may be sent and summed in bfloat16 or wider, within the bound.
A program may use at most 128 MiB of HBM per device.

```python
import math
import jax
import jax.numpy as jnp
from jax import lax

D = 768
CB = 128
RB = 128
CANDS = 4
BLK_OWN = 32
RB_DEV = 16
OWNERS = 16
SLABS = 16
BPD = 2
NB = 512
K = 65536
ROWS = 524288


def draw_candidates(key, part):
    total = RB_DEV * SLABS * OWNERS
    spacing = BLK_OWN // CANDS
    first_draw = jax.random.randint(jax.random.fold_in(key, 1), (total,), 0, BLK_OWN)
    second_draw = jax.random.randint(jax.random.fold_in(key, 2), (total,), 0, BLK_OWN)
    base_ids = first_draw * second_draw // BLK_OWN
    position = jnp.arange(total, dtype=jnp.int32) % RB_DEV
    base_ids = jnp.where(position == 0, BLK_OWN - 1, jnp.where(position == 1, 0, base_ids))
    offsets = jax.random.randint(jax.random.fold_in(key, 3), (total, CANDS), 0, spacing)
    slot_index = jnp.arange(CANDS, dtype=jnp.int32)[None, :]
    offsets = jnp.where(slot_index == 0, 0, offsets)
    group_ids = (base_ids[:, None] + slot_index * spacing + offsets) % BLK_OWN
    owner_index = jnp.arange(total, dtype=jnp.int32) // RB_DEV % OWNERS
    holder = group_ids // BPD
    return ((holder * OWNERS + owner_index[:, None]) * BPD + group_ids % BPD).astype(jnp.int32)


def level_of(key, dims, cuts, low, top_value):
    loudness = 1.0
    for axis_at, shards_of in cuts:
        draws = jax.random.uniform(jax.random.fold_in(jax.random.fold_in(key, 6), axis_at), (shards_of,), jnp.float32, low / len(cuts), top_value / len(cuts))
        loudness = loudness * jnp.repeat(jnp.exp(draws), dims[axis_at] // shards_of).reshape((-1,) + (1,) * (len(dims) - 1 - axis_at))
    return loudness


def bell_draw(rng, shape, scale, limit, shards=(), kind=jnp.bfloat16):
    result = jax.random.normal(rng, shape, jnp.float32) * scale
    if len(shards) > 0:
        result = level_of(rng, shape, shards, -0.22, 0.18) * result
    return jnp.clip(result, min=-limit, max=limit).astype(kind)


def setup_inputs(seed: int = 0) -> dict:
    key_of = jax.random.split(jax.random.key(seed), 6)
    return {
        "points": bell_draw(key_of[0], (ROWS, D), 1.0, 6.0, ((0, 256),)),
        "candidates": draw_candidates(jax.random.fold_in(key_of[5], 71), 0),
        "means": bell_draw(key_of[2], (K, D), 0.1, 0.59765625, ((0, 256),)),
        "inv_var": jnp.clip(1.0 + 0.1 * jax.random.normal(key_of[3], (K, D), jnp.float32), 0.5, 1.5).astype(jnp.bfloat16),
        "log_weight": jnp.clip(-12.0 + 3.0 * jax.random.uniform(key_of[4], (K,), jnp.float32) ** level_of(key_of[4], (K,), ((0, 256),), -0.2, 0.2), -12.0, -9.0).astype(jnp.bfloat16),
    }


def component_consts(mean_values, inv_values, log_values):
    mean_f = mean_values.astype(jnp.float32)
    inv_f = inv_values.astype(jnp.float32)
    return (log_values.astype(jnp.float32) + 0.5 * jnp.sum(jnp.log(inv_f), axis=1)
            - 0.5 * jnp.sum(inv_f * mean_f * mean_f, axis=1) - 0.5 * D * math.log(2.0 * math.pi))


def block_terms(row_block, chosen_ids, scaled, inverse, constants):
    row_f = row_block.astype(jnp.float32)
    squares = (row_f * row_f).astype(jnp.bfloat16)
    square_f = squares.astype(jnp.float32)
    chosen_scaled = scaled[chosen_ids].astype(jnp.float32)
    chosen_inverse = inverse[chosen_ids].astype(jnp.float32)
    chosen_consts = constants[chosen_ids]
    linear = jnp.einsum('grd,gskd->grsk', row_f, chosen_scaled, precision=lax.Precision.HIGHEST)
    quadratic = jnp.einsum('grd,gskd->grsk', square_f, chosen_inverse, precision=lax.Precision.HIGHEST)
    densities = chosen_consts[:, None] + linear - 0.5 * quadratic
    row_peak = jnp.max(densities, axis=(2, 3))
    normalizer = row_peak + jnp.log(jnp.sum(jnp.exp(densities - row_peak[:, :, None, None]), axis=(2, 3)))
    responsibility = jnp.exp(densities - normalizer[:, :, None, None]).astype(jnp.bfloat16)
    weights = responsibility.astype(jnp.float32)
    counts = jnp.sum(weights, axis=1)
    first_moment = jnp.einsum('grsk,grd->gskd', weights, row_f, precision=lax.Precision.HIGHEST)
    second_moment = jnp.einsum('grsk,grd->gskd', weights, square_f, precision=lax.Precision.HIGHEST)
    return normalizer, counts, first_moment, second_moment


def reference(points, candidates, means, inv_var, log_weight):
    scaled = (inv_var.astype(jnp.float32) * means.astype(jnp.float32)).astype(jnp.bfloat16).reshape(NB, CB, D)
    inverse = inv_var.reshape(NB, CB, D)
    constants = component_consts(means, inv_var, log_weight).reshape(NB, CB)
    device_rows = points.reshape(SLABS * OWNERS, RB_DEV, RB, D)
    device_ids = candidates.reshape(SLABS * OWNERS, RB_DEV, CANDS).astype(jnp.int32)
    owner_seq = jnp.arange(SLABS * OWNERS, dtype=jnp.int32) % OWNERS
    group_index = jnp.arange(BLK_OWN, dtype=jnp.int32)

    def per_device(running, inputs):
        row_block, chosen_ids, owner_index = inputs
        normalizer, counts, first_part, second_part = block_terms(row_block, chosen_ids, scaled, inverse, constants)
        local_ids = ((chosen_ids // (OWNERS * BPD)) * BPD + chosen_ids % BPD).reshape(-1)
        part_counts = jnp.zeros((BLK_OWN, CB), jnp.float32).at[local_ids].add(counts.reshape(-1, CB))
        part_first = jnp.zeros((BLK_OWN, CB, D), jnp.float32).at[local_ids].add(first_part.reshape(-1, CB, D))
        part_second = jnp.zeros((BLK_OWN, CB, D), jnp.float32).at[local_ids].add(second_part.reshape(-1, CB, D))
        rounded = lax.optimization_barrier((part_counts.astype(jnp.bfloat16), part_first.astype(jnp.bfloat16),
                                            part_second.astype(jnp.bfloat16)))
        global_ids = ((group_index // BPD) * OWNERS + owner_index) * BPD + group_index % BPD
        running = (running[0].at[global_ids].add(rounded[0].astype(jnp.float32)),
                   running[1].at[global_ids].add(rounded[1].astype(jnp.float32)),
                   running[2].at[global_ids].add(rounded[2].astype(jnp.float32)))
        return running, normalizer.reshape(-1)

    initial = (jnp.zeros((NB, CB), jnp.float32), jnp.zeros((NB, CB, D), jnp.float32),
               jnp.zeros((NB, CB, D), jnp.float32))
    totals, normalizers = lax.scan(per_device, initial, (device_rows, device_ids, owner_seq))
    loglik = normalizers.reshape(-1) / D
    return (totals[0].reshape(K), totals[1].reshape(K, D), totals[2].reshape(K, D), loglik)
```

```python
import functools
import math

import jax
import jax.numpy as jnp
from jax import lax
from jax.experimental import pallas as pl
from jax.experimental.pallas import tpu as pltpu
from jax.sharding import PartitionSpec as P

CB = 128
RB = 128
CANDS = 4
MESH = pl.DeviceIdType.MESH
NT = (((1,), (1,)), ((), ()))


def remote(src, dst, sems, at, dev):
    send, recv = sems
    return pltpu.make_async_remote_copy(
        src_ref=src,
        dst_ref=dst,
        send_sem=send.at[at],
        recv_sem=recv.at[at],
        device_id={"dp": dev},
        device_id_type=MESH,
    )


def kernel(
    chips,
    cand,
    logw,
    points,
    means,
    inv_var,
    counts_out,
    first_out,
    second_out,
    loglik_out,
    mv,
    iv,
    x,
    g,
    gc,
    slots,
    resp,
    wt,
    acc,
    acc_c,
    ss,
    ss_c,
    sr,
    sr_c,
    rp,
    rp_c,
    rm,
    rm_c,
    in_sem,
    ap_s,
    ap_r,
    am_s,
    am_r,
    as_s,
    as_r,
    rs_s,
    rs_r,
    rp_s,
    rp_r,
    rm_s,
    rm_r,
):
    feat = means.shape[1]
    blocks = cand.shape[0]
    rows = blocks * RB
    dp = lax.axis_index("dp")
    comp = lax.axis_index("comp")
    owners = lax.axis_size("comp")
    n_dp = 2 * chips
    z, c = dp // 2, lax.rem(dp, 2)
    right = lax.rem(dp + 2, n_dp)
    left = lax.rem(dp + n_dp - 2, n_dp)
    sib = dp + 1 - 2 * c

    def share(offset, core):
        return 2 * lax.rem(z + offset + chips, chips) + core

    load_m = pltpu.make_async_copy(means, mv, in_sem.at[0])
    load_i = pltpu.make_async_copy(inv_var, iv, in_sem.at[1])
    load_p = pltpu.make_async_copy(points, x.at[:, pl.ds(0, feat)], in_sem.at[2])
    load_m.start()
    load_i.start()
    load_p.start()

    barrier = pltpu.get_barrier_semaphore()
    for dev in (left, right, sib):
        pl.semaphore_signal(barrier, inc=1, device_id={"dp": dev}, device_id_type=MESH)

    sent = []

    def send(src, src_c, dst, dst_c, sems, at, dev):
        one = remote(src, dst, sems, (*at, 0), dev)
        two = remote(src_c, dst_c, sems, (*at, 1), dev)
        one.start()
        two.start()
        sent.extend((one, two))

    def got(dst, dst_c, sems, at, dev):
        remote(dst, dst, sems, (*at, 0), dev).wait_recv()
        remote(dst_c, dst_c, sems, (*at, 1), dev).wait_recv()

    plus, minus, across = (ap_s, ap_r), (am_s, am_r), (as_s, as_r)

    def pass_on(sh, j, sems, at, dev):
        send(g.at[sh, j], gc.at[sh, j], g.at[sh, j], gc.at[sh, j], sems, (at, j), dev)

    def arrive(sh, j, sems, at, dev):
        got(g.at[sh, j], gc.at[sh, j], sems, (at, j), dev)

    load_m.wait()
    load_i.wait()
    for j in range(2):
        part = pl.ds(j * CB, CB)
        m = mv[part, :].astype(jnp.float32)
        v = iv[part, :].astype(jnp.float32)
        scaled = v * m
        g[dp, j, :, pl.ds(0, feat)] = scaled.astype(jnp.bfloat16)
        g[dp, j, :, pl.ds(feat, feat)] = (-0.5 * v).astype(jnp.bfloat16)
        term = 0.5 * jnp.sum(jnp.log(v) - scaled * m, axis=1, keepdims=True)
        flat = jnp.transpose(jnp.broadcast_to(term, (CB, CB)))[0:8, :]
        weight = logw[pl.ds(j, 1), :].astype(jnp.float32)
        gc[dp, j] = flat + weight - 0.5 * feat * math.log(2.0 * math.pi)
        if j == 0:
            pl.semaphore_wait(barrier, 3)
        pass_on(dp, j, plus, 0, right)
        pass_on(dp, j, minus, 0, left)
        pass_on(dp, j, across, 0, sib)

    load_p.wait()

    def square(i, carry):
        at = pl.ds(pl.multiple_of(i * RB, RB), RB)
        p = x[at, pl.ds(0, feat)].astype(jnp.float32)
        x[at, pl.ds(feat, feat)] = (p * p).astype(jnp.bfloat16)
        return carry

    lax.fori_loop(0, blocks, square, 0)

    def density(sh):
        base = (sh * owners + comp) * 2
        cols = [
            jnp.transpose(jnp.broadcast_to(gc[sh, j, 0:1, :], (CB, CB))) for j in range(2)
        ]
        lhs = g.at[sh]

        def body(i, carry):
            at = pl.ds(pl.multiple_of(i * 2 * RB, 2 * RB), 2 * RB)
            d = lax.dot_general(
                lhs[...].reshape(2 * CB, 2 * feat),
                x[at, :],
                NT,
                preferred_element_type=jnp.float32,
            )
            for r in range(2):
                n = 2 * i + r
                low = d[0:CB, r * RB : (r + 1) * RB] + cols[0]
                high = d[CB : 2 * CB, r * RB : (r + 1) * RB] + cols[1]
                for s in range(CANDS):
                    named = cand[n, s]
                    slots[n, s] = jnp.where(
                        named == base, low, jnp.where(named == base + 1, high, slots[n, s])
                    )
            return carry

        lax.fori_loop(0, blocks // 2, body, 0)

    far = chips // 2
    across_plus, across_minus = 1, 1 + far

    def hop_blocks(h, first):
        return (0, 1) if h < far - 1 else ((0,) if first else (1,))

    def receive(h, j):
        up, down = share(-1 - h, c), share(1 + h, c)
        if j in hop_blocks(h, True):
            arrive(up, j, plus, h, right)
            if h + 1 < far and j in hop_blocks(h + 1, True):
                pass_on(up, j, plus, h + 1, right)
            pass_on(up, j, across, across_plus + h, sib)
        if j in hop_blocks(h, False):
            arrive(down, j, minus, h, left)
            if h + 1 < far and j in hop_blocks(h + 1, False):
                pass_on(down, j, minus, h + 1, left)
            pass_on(down, j, across, across_minus + h, sib)

    def from_sib(h, first):
        sh = share(-1 - h, 1 - c) if first else share(1 + h, 1 - c)
        for j in hop_blocks(h, first):
            arrive(sh, j, across, (across_plus if first else across_minus) + h, sib)
        return sh

    density(dp)
    for j in range(2):
        arrive(sib, j, across, 0, sib)
    receive(0, 0)
    density(sib)
    receive(0, 1)
    for h in range(far - 1):
        density(share(-1 - h, c))
        density(share(1 + h, c))
        if h + 1 < far - 1:
            receive(h + 1, 0)
        density(from_sib(h, True))
        if h + 1 == far - 1:
            receive(h + 1, 0)
            receive(h + 1, 1)
        density(from_sib(h, False))
        if h + 1 < far - 1:
            receive(h + 1, 1)
    density(share(far, c))
    from_sib(far - 1, False)
    density(from_sib(far - 1, True))

    def soften(n, carry):
        d = slots[n]
        peak = jnp.max(jnp.max(d, axis=0), axis=0, keepdims=True)
        e = jnp.exp(d - peak[None])
        total = jnp.sum(jnp.sum(e, axis=0), axis=0, keepdims=True)
        loglik_out[pl.ds(n, 1), :] = (peak + jnp.log(total)) / feat
        resp[n, pl.ds(0, CANDS)] = (e * (1.0 / total)[None]).astype(jnp.bfloat16)
        resp[n, CANDS] = jnp.zeros((CB, RB), jnp.bfloat16)
        return carry

    lax.fori_loop(0, blocks, soften, 0)

    ones = jnp.ones((16, rows), jnp.bfloat16)
    width = 256 if (2 * feat) % 256 == 0 else 128

    def moments(sh, dst, dst_c):
        base = (sh * owners + comp) * 2

        def fill(n, carry):
            for j in range(2):
                at = jnp.int32(CANDS)
                for s in range(CANDS):
                    at = jnp.where(cand[n, s] == base + j, s, at)
                wt[pl.ds(j * CB, CB), pl.ds(pl.multiple_of(n * RB, RB), RB)] = resp[n, at]
            return carry

        lax.fori_loop(0, blocks, fill, 0)
        total = lax.dot_general(ones, wt[...], NT, preferred_element_type=jnp.float32)
        for j in range(2):
            dst_c[j] = total[:, j * CB : (j + 1) * CB].astype(dst_c.dtype)

        def body(k, carry):
            cut = pl.ds(pl.multiple_of(k * width, width), width)
            m = jnp.dot(wt[...], x[:, cut], preferred_element_type=jnp.float32)
            for j in range(2):
                dst[j, :, cut] = m[j * CB : (j + 1) * CB, :].astype(dst.dtype)
            return carry

        lax.fori_loop(0, 2 * feat // width, body, 0)

    plus, minus, across = (rp_s, rp_r), (rm_s, rm_r), (rs_s, rs_r)
    order = [(far, 0)]
    for away in range(far - 1, 0, -1):
        order += [(away, 1), (away, -1)]
    order += [(0, 0)]
    for i, (away, way) in enumerate(order):
        target = way * away if way else away
        moments(share(target, 1 - c), ss.at[i], ss_c.at[i])
        for j in range(2):
            send(ss.at[i, j], ss_c.at[i, j], sr.at[i, j], sr_c.at[i, j], across, (i, j), sib)
        moments(share(target, c), acc, acc_c)
        level = far - away
        for j in (0, 1) if way < 0 else (1, 0):
            got(sr.at[i, j], sr_c.at[i, j], across, (i, j), sib)
            terms = [(sr.at[i, j], sr_c.at[i, j])]
            if away < far and way >= 0 and (level > 1 or j == 0):
                got(rp.at[level - 1, j], rp_c.at[level - 1, j], plus, (level - 1, j), right)
                terms.append((rp.at[level - 1, j], rp_c.at[level - 1, j]))
            if away < far and way <= 0 and (level > 1 or j == 1):
                got(rm.at[level - 1, j], rm_c.at[level - 1, j], minus, (level - 1, j), left)
                terms.append((rm.at[level - 1, j], rm_c.at[level - 1, j]))
            part = pl.ds(j * CB, CB)
            count = acc_c[j]
            for _, t in terms:
                count = count + t[...].astype(jnp.float32)
            if away:
                sr_c[i, j] = count.astype(jnp.bfloat16)
            else:
                counts_out[pl.ds(j, 1), :] = count[0:1, :]

            def add(r, carry, j=j, i=i, terms=terms, away=away):
                here = pl.ds(pl.multiple_of(r * 16, 16), 16)
                t = acc[j, here, :]
                for term, _ in terms:
                    t = t + term[here, :].astype(jnp.float32)
                if away:
                    sr[i, j, here, :] = t.astype(jnp.bfloat16)
                else:
                    there = pl.ds(pl.multiple_of(j * CB + r * 16, 16), 16)
                    first_out[there, :] = t[:, :feat]
                    second_out[there, :] = t[:, feat:]
                return carry

            lax.fori_loop(0, CB // 16, add, 0)
            if away == 0:
                continue
            up = way > 0 or (way == 0 and j == 0)
            dst, dst_c = (rp, rp_c) if up else (rm, rm_c)
            send(
                sr.at[i, j],
                sr_c.at[i, j],
                dst.at[level, j],
                dst_c.at[level, j],
                plus if up else minus,
                (level, j),
                right if up else left,
            )

    for copy in sent:
        copy.wait_send()


def on_device(points, candidates, means, inv_var, log_weight):
    rows, feat = points.shape
    blocks = candidates.shape[0]
    n_dp = lax.axis_size("dp")
    chips = n_dp // 2
    far = chips // 2
    any_space = pl.BlockSpec(memory_space=pl.ANY)
    vmem = pl.BlockSpec(memory_space=pltpu.VMEM)
    bf16, f32 = jnp.bfloat16, jnp.float32
    sem = pltpu.SemaphoreType.DMA
    wide = 2 * feat
    counts, first, second, loglik = pl.pallas_call(
        functools.partial(kernel, chips),
        out_shape=(
            jax.ShapeDtypeStruct((2, CB), f32),
            jax.ShapeDtypeStruct((2 * CB, feat), f32),
            jax.ShapeDtypeStruct((2 * CB, feat), f32),
            jax.ShapeDtypeStruct((blocks, RB), f32),
        ),
        in_specs=[
            pl.BlockSpec(memory_space=pltpu.SMEM),
            vmem,
            any_space,
            any_space,
            any_space,
        ],
        out_specs=(vmem, vmem, vmem, vmem),
        scratch_shapes=[
            pltpu.VMEM((2 * CB, feat), bf16),
            pltpu.VMEM((2 * CB, feat), bf16),
            pltpu.VMEM((rows, wide), bf16),
            pltpu.VMEM((n_dp, 2, CB, wide), bf16),
            pltpu.VMEM((n_dp, 2, 8, CB), f32),
            pltpu.VMEM((blocks, CANDS, CB, RB), f32),
            pltpu.VMEM((blocks, CANDS + 1, CB, RB), bf16),
            pltpu.VMEM((2 * CB, rows), bf16),
            pltpu.VMEM((2, CB, wide), f32),
            pltpu.VMEM((2, 16, CB), f32),
            pltpu.VMEM((chips, 2, CB, wide), bf16),
            pltpu.VMEM((chips, 2, 16, CB), bf16),
            pltpu.VMEM((chips, 2, CB, wide), bf16),
            pltpu.VMEM((chips, 2, 16, CB), bf16),
            pltpu.VMEM((far, 2, CB, wide), bf16),
            pltpu.VMEM((far, 2, 16, CB), bf16),
            pltpu.VMEM((far, 2, CB, wide), bf16),
            pltpu.VMEM((far, 2, 16, CB), bf16),
            sem((3,)),
            sem((far, 2, 2)),
            sem((far, 2, 2)),
            sem((far, 2, 2)),
            sem((far, 2, 2)),
            sem((chips + 1, 2, 2)),
            sem((chips + 1, 2, 2)),
            sem((chips, 2, 2)),
            sem((chips, 2, 2)),
            sem((far, 2, 2)),
            sem((far, 2, 2)),
            sem((far, 2, 2)),
            sem((far, 2, 2)),
        ],
        compiler_params=pltpu.CompilerParams(
            collective_id=0, has_side_effects=True, vmem_limit_bytes=60 * 2**20
        ),
        cost_estimate=pl.CostEstimate(
            flops=4 * rows * n_dp * 2 * CB * wide,
            bytes_accessed=(rows + 8 * CB) * feat * 2,
            transcendentals=rows * CANDS * CB,
        ),
    )(candidates, log_weight.reshape(2, CB), points, means, inv_var)
    return (counts.reshape(-1), first, second, loglik.reshape(-1))


def solution(mesh):
    rows = P(("dp", "comp"))
    wide = P(("dp", "comp"), None)
    return jax.shard_map(
        on_device,
        mesh=mesh,
        in_specs=(wide, wide, wide, wide, rows),
        out_specs=(rows, wide, wide, rows),
        check_vma=False,
    )
```

```python
import functools
import math

import jax
import jax.numpy as jnp
from jax import lax
from jax.experimental import pallas as pl
from jax.experimental.pallas import tpu as pltpu
from jax.sharding import PartitionSpec as P

CB = 128
RB = 128
CANDS = 4
EXTRA = 16
ROW_CHUNK = 1024
MESH = pl.DeviceIdType.MESH
BF16, F32 = jnp.bfloat16, jnp.float32


def kernel(
    chips,
    cand,
    logw,
    points,
    means,
    inv_var,
    counts_out,
    first_out,
    second_out,
    loglik_out,
    mv,
    iv,
    x,
    xt,
    g,
    slots,
    resp,
    wr,
    acc,
    ss,
    sr,
    rr,
    in_sem,
    ag_s,
    ag_r,
    as_s,
    as_r,
    rs_s,
    rs_r,
    rr_s,
    rr_r,
):
    feat = means.shape[1]
    wide = 2 * feat
    blocks = cand.shape[1]
    rows = blocks * RB
    dp = lax.axis_index("dp")
    comp = lax.axis_index("comp")
    owners = lax.axis_size("comp")
    n_dp = 2 * chips
    far = chips // 2
    z, c = dp // 2, lax.rem(dp, 2)
    right = lax.rem(dp + 2, n_dp)
    left = lax.rem(dp + n_dp - 2, n_dp)
    sib = dp + 1 - 2 * c
    ring = (right, left)
    halves = ((0, feat), (feat, feat + EXTRA))

    def share(offset, core):
        return 2 * lax.rem(z + offset + chips, chips) + core

    def remote(src, dst, sems, at, dev):
        return pltpu.make_async_remote_copy(
            src_ref=src,
            dst_ref=dst,
            send_sem=sems[0].at[at],
            recv_sem=sems[1].at[at],
            device_id={"dp": dev},
            device_id_type=MESH,
        )

    load_m = pltpu.make_async_copy(means, mv, in_sem.at[0])
    load_i = pltpu.make_async_copy(inv_var, iv, in_sem.at[1])
    load_p = pltpu.make_async_copy(points, x.at[:, pl.ds(0, feat)], in_sem.at[2])
    load_m.start()
    load_i.start()
    load_p.start()

    barrier = pltpu.get_barrier_semaphore()
    for dev in (left, right, sib):
        pl.semaphore_signal(barrier, inc=1, device_id={"dp": dev}, device_id_type=MESH)

    ring_sems, across = (ag_s, ag_r), (as_s, as_r)

    def start(ref, sems, at, dev):
        remote(ref, ref, sems, at, dev).start()

    def arrive(ref, sems, at):
        remote(ref, ref, sems, at, sib).wait_recv()

    def half(sh, j, p):
        return g.at[sh, j, pl.ds(halves[p][0], halves[p][1])]

    def own_block(j):
        part = pl.ds(j * CB, CB)
        m = mv[part, :].astype(F32)
        v = iv[part, :].astype(F32)
        scaled = v * m
        g[dp, j, pl.ds(0, feat), :] = jnp.transpose(scaled.astype(BF16))
        g[dp, j, pl.ds(feat, feat), :] = jnp.transpose((-0.5 * v).astype(BF16))
        term = jnp.log(v) - scaled * m
        folded = term[:, 0:CB]
        for k in range(1, feat // CB):
            folded = folded + term[:, k * CB : (k + 1) * CB]
        const = 0.5 * jnp.sum(jnp.transpose(folded), axis=0, keepdims=True)
        const = logw[pl.ds(j, 1), :].astype(F32) + const - 0.5 * feat * math.log(2.0 * math.pi)
        high = const.astype(BF16).astype(F32)
        mid = (const - high).astype(BF16).astype(F32)
        low = const - high - mid
        at = lax.broadcasted_iota(jnp.int32, (EXTRA, CB), 0)
        tile = jnp.where(at == 0, high, jnp.where(at == 1, mid, jnp.where(at == 2, low, 0.0)))
        g[dp, j, pl.ds(wide, EXTRA), :] = tile.astype(BF16)
        if j == 0:
            pl.semaphore_wait(barrier, 3)
        start(g.at[dp, j], ring_sems, (0, 0, j), right)
        start(g.at[dp, j], ring_sems, (1, 0, j), left)
        start(g.at[dp, j], across, (0, j), sib)

    load_m.wait()
    load_i.wait()
    own_block(0)
    load_p.wait()

    def spread(i, carry):
        at = pl.ds(pl.multiple_of(i * RB, RB), RB)
        p = x[at, pl.ds(0, feat)]
        pf = p.astype(F32)
        q = (pf * pf).astype(BF16)
        x[at, pl.ds(feat, feat)] = q
        xt[pl.ds(0, feat), at] = jnp.transpose(p)
        xt[pl.ds(feat, feat), at] = jnp.transpose(q)
        xt[pl.ds(wide, EXTRA), at] = jnp.ones((EXTRA, RB), BF16)
        return carry

    lax.fori_loop(0, blocks, spread, 0)
    own_block(1)

    chunk = min(ROW_CHUNK, rows)

    def keep(i, d, bases, consts):
        for r in range(chunk // RB):
            n = i * (chunk // RB) + r
            here = slice(r * RB, (r + 1) * RB)
            low = d[here, 0:CB] + consts[0]
            high = d[here, CB : 2 * CB] + consts[1]
            for s in range(CANDS):
                named = cand[s, n]
                slots[n, s] = jnp.where(
                    named == bases[0], low, jnp.where(named == bases[1], high, slots[n, s])
                )

    def offsets_of(pair):
        bases, consts = [], []
        for sh, j in pair:
            bases.append((sh * owners + comp) * 2 + j)
            tile = g[sh, j, pl.ds(wide, EXTRA), :].astype(F32)
            consts.append(jnp.sum(tile, axis=0, keepdims=True))
        return bases, consts

    def density(pair):
        bases, consts = offsets_of(pair)
        (sh_a, j_a), (sh_b, j_b) = pair

        def body(i, carry):
            at = pl.ds(pl.multiple_of(i * chunk, chunk), chunk)
            cut = pl.ds(0, wide)
            w = jnp.concatenate([g[sh_a, j_a, cut, :], g[sh_b, j_b, cut, :]], axis=1)
            keep(i, jnp.dot(x[at, :], w, preferred_element_type=F32), bases, consts)
            return carry

        lax.fori_loop(0, rows // chunk, body, 0)

    def density_half(sh, p, store):
        cut = pl.ds(pl.multiple_of(p * feat, feat), feat)

        def body(i, carry):
            at = pl.ds(pl.multiple_of(i * chunk, chunk), chunk)
            kept = pl.ds(pl.multiple_of(store * rows + i * chunk, chunk), chunk)
            w = jnp.concatenate([g[sh, 0, cut, :], g[sh, 1, cut, :]], axis=1)
            d = jnp.dot(x[at, cut], w, preferred_element_type=F32)

            @pl.when(p == 0)
            def _():
                acc[kept, :] = d

            @pl.when(p == 1)
            def _():
                keep(i, d + acc[kept, :], *offsets_of(((sh, 0), (sh, 1))))

            return carry

        lax.fori_loop(0, rows // chunk, body, 0)

    def block_of(way, h, e):
        return e if way == 0 else jnp.where(h == 0, e, 1 - e)

    def hop_share(way, h, core):
        return share(-1 - h if way == 0 else 1 + h, core)

    def pair_of(h, e, core):
        return [(hop_share(way, h, core), block_of(way, h, e)) for way in range(2)]

    def receive(h, e):
        for way, (sh, j) in enumerate(pair_of(h, e, c)):
            arrive(g.at[sh, j], ring_sems, (way, h, j))

            @pl.when(h + 1 < far - 1)
            def _(way=way, sh=sh, j=j):
                start(g.at[sh, j], ring_sems, (way, h + 1, j), ring[way])

            @pl.when((h + 1 == far - 1) & (j == way))
            def _(way=way, sh=sh):
                for p in range(2):
                    start(half(sh, way, p), ring_sems, (way, far - 1, p), ring[way])

            start(g.at[sh, j], across, (1 + way * far + h, j), sib)

    def early(t, carry):
        h, e = (t + 1) // 2 - 1, lax.rem(t + 1, 2)

        def one(k, carry):
            core = jnp.where(k == 0, c, 1 - c)
            own = jnp.where(k == 0, dp, sib)
            pair = [
                (jnp.where(t == 0, own, sh), jnp.where(t == 0, way, j))
                for way, (sh, j) in enumerate(pair_of(h, e, core))
            ]

            @pl.when(k == 1)
            def _():
                for way, (sh, j) in enumerate(pair):
                    at = jnp.where(t == 0, 0, 1 + way * far + h)
                    arrive(g.at[sh, j], across, (at, j))

            density(pair)

            @pl.when((k == 0) & (t < 2 * far - 2))
            def _():
                receive(t // 2, lax.rem(t, 2))

            return carry

        lax.fori_loop(0, 2, one, 0)
        return carry

    lax.fori_loop(0, 2 * far - 1, early, 0)

    def late(p, carry):
        sh = share(far, c)
        for part in range(2):

            @pl.when(p == part)
            def _(part=part):
                for way in range(2):
                    arrive(half(sh, way, part), ring_sems, (way, far - 1, part))
                    start(half(sh, way, part), across, (1 + way * far + far - 1, part), sib)

        def one(k, carry):
            target = share(far, jnp.where(k == 0, c, 1 - c))
            for part in range(2):

                @pl.when((k == 1) & (p == part))
                def _(part=part):
                    for way in range(2):
                        at = (1 + way * far + far - 1, part)
                        arrive(half(target, way, part), across, at)

            density_half(target, p, k)
            return carry

        lax.fori_loop(0, 2, one, 0)
        return carry

    lax.fori_loop(0, 2, late, 0)

    def soften(n):
        d = [slots[n, s] for s in range(CANDS)]
        peak = jnp.max(
            jnp.maximum(jnp.maximum(d[0], d[1]), jnp.maximum(d[2], d[3])), axis=1, keepdims=True
        )
        e = [jnp.exp(v - peak) for v in d]
        total = jnp.sum((e[0] + e[1]) + (e[2] + e[3]), axis=1, keepdims=True)
        scale = 1.0 / total
        for s in range(CANDS):
            resp[n, s] = (e[s] * scale).astype(BF16)
        resp[n, CANDS] = jnp.zeros((RB, CB), BF16)
        slots[n, 0] = jnp.broadcast_to(peak + jnp.log(total), (RB, CB))

    def soften_some(i, carry):
        for k in range(4):
            soften(4 * i + k)
        return carry

    lax.fori_loop(0, blocks // 4, soften_some, 0)

    def sent():
        for way in range(2):
            for h in range(far):
                for p in range(2):
                    ref = g.at[0, 0] if h < far - 1 else half(0, 0, p)
                    remote(ref, ref, ring_sems, (way, h, p), sib).wait_send()
                    remote(ref, ref, across, (1 + way * far + h, p), sib).wait_send()
        for j in range(2):
            remote(g.at[0, 0], g.at[0, 0], across, (0, j), sib).wait_send()

    room = acc.shape[0] // 4
    sum_sems, pair_sems = (rr_s, rr_r), (rs_s, rs_r)
    part = feat // 2

    def fill(k, lv):
        way, core = k // 2, jnp.where(lax.rem(k, 2) == 0, 1 - c, c)
        sh = share(jnp.where(way == 0, far - lv, lv - far), core)
        base = (sh * owners + comp) * 2

        def body(n, carry):
            for j in range(2):
                pick = jnp.int32(CANDS)
                for s in range(CANDS):
                    pick = jnp.where(cand[s, n] == base + j, s, pick)
                here = pl.ds(pl.multiple_of(n * RB, RB), RB)
                wr[k, here, pl.ds(j * CB, CB)] = resp[n, pick]
            return carry

        lax.fori_loop(0, blocks, body, 0)

    def place(sub):
        return pl.ds(pl.multiple_of(sub * part, part), part) if sub is not None else pl.ds(feat, EXTRA)

    def ss_copy(s, way, q, sub):
        at = (2 * s + way, 2 if sub is None else sub)
        return remote(
            ss.at[2 * way + q, place(sub)], sr.at[2 * s + way, place(sub)], pair_sems, at, sib
        )

    def rr_copy(s, way, q, sub):
        lv = (s + 1) // 2
        at = (way, lv, q, 2 if sub is None else sub)
        return remote(
            sr.at[2 * s + way, place(sub)], rr.at[way, lv, q, place(sub)], sum_sems, at, ring[way]
        )

    def on_way(way, act):
        for w in range(2):

            @pl.when(way == w)
            def _(w=w):
                act(w)

    def step(s, carry):
        lv, e = (s + 1) // 2, lax.rem(s + 1, 2)

        @pl.when((s == 0) | (e == 0))
        def _():
            def body(k, carry):
                fill(k, lv)
                return carry

            lax.fori_loop(0, 4, body, 0)

        def one(k, carry):
            core, sub, way = lax.rem(k // 2, 2), k // 4, lax.rem(k, 2)
            q = jnp.where(e == 1, way, 1 - way)
            slot = 2 * way + q

            def product(low, size):
                return jnp.dot(
                    xt[pl.ds(low, size), :], wr[2 * way + core], preferred_element_type=F32
                )

            def put(value, where):
                @pl.when(core == 0)
                def _():
                    @pl.when(s >= 2)
                    def _():
                        ss_copy(s - 2, way, q, where).wait_send()

                    ss[slot, place(where), :] = value.astype(BF16)
                    ss_copy(s, way, q, where).start()

                @pl.when(core == 1)
                def _():
                    start = sub * part if where is not None else feat
                    acc[pl.ds(pl.multiple_of(slot * room + start, 16), value.shape[0]), :] = value

            put(product(pl.multiple_of(q * feat + sub * part, part), part), sub)

            @pl.when((q == 1) & (sub == 1))
            def _():
                put(product(wide, EXTRA), None)

            def combine(where, tile, count):
                ss_copy(s, way, q, where).wait_recv()
                level = lv - 1

                def add(extra):
                    def body(r, carry):
                        start = (sub * part if where is not None else feat) + r * tile
                        start = pl.multiple_of(start, 16)
                        here = pl.ds(start, tile)
                        t = acc[pl.ds(pl.multiple_of(slot * room + start, 16), tile), :]
                        t = t + sr[2 * s + way, here, :].astype(F32)
                        if extra:
                            t = t + rr[way, level, q, here, :].astype(F32)
                        sr[2 * s + way, here, :] = t.astype(BF16)
                        return carry

                    lax.fori_loop(0, count, body, 0)

                @pl.when(s < 2)
                def _():
                    add(False)

                @pl.when((s >= 2) & (lv < far))
                def _():
                    before = jnp.where(s == 2, 0, s - 2)
                    on_way(way, lambda w: rr_copy(before, w, q, where).wait_recv())
                    add(True)

                @pl.when(lv < far)
                def _():
                    on_way(way, lambda w: rr_copy(s, w, q, where).start())

            @pl.when(core == 1)
            def _():
                count = max(k for k in range(1, 9) if part // 16 % k == 0)
                combine(sub, 16 * count, part // (16 * count))

                @pl.when((q == 1) & (sub == 1))
                def _():
                    combine(None, EXTRA, 1)

            return carry

        lax.fori_loop(0, 8, one, 0)

        @pl.when(s == 1)
        def _():
            def out(n, carry):
                norm = jnp.transpose(slots[n, 0])[0:1, :]
                loglik_out[pl.ds(n, 1), :] = norm / feat
                return carry

            lax.fori_loop(0, blocks, out, 0)

        return carry

    lax.fori_loop(0, 2 * far, step, 0)

    last = 2 * far - 1

    def final_of(q, start, size):
        way = 1 - q
        t = acc[pl.ds((2 * way + q) * room + start, size), :]
        t = t + sr[2 * last + way, pl.ds(start, size), :].astype(F32)
        for w in range(2):
            t = t + rr[w, far - 1, q, pl.ds(start, size), :].astype(F32)
        return t

    def done(q, sub):
        for w in range(2):
            rr_copy(last - 1 if q == w else last - 2, w, q, sub).wait_recv()

    for sub in range(2):
        for q in range(2):
            done(q, sub)
            out = second_out if q else first_out
            edges = list(range(sub * part, (sub + 1) * part, min(CB, part)))
            for low in edges:
                t = final_of(q, low, min(CB, part))
                out[:, pl.ds(low, min(CB, part))] = jnp.transpose(t)
    done(1, None)
    t = final_of(1, feat, EXTRA)
    for j in range(2):
        counts_out[pl.ds(j, 1), :] = t[0:1, j * CB : (j + 1) * CB]

    sent()
    for s in range(2 * far):
        for way in range(2):
            q = way if s % 2 == 0 else 1 - way
            for sub in (0, 1) if q == 0 else (0, 1, None):
                if s >= last - 1:
                    ss_copy(s, way, q, sub).wait_send()
                if s < last:
                    rr_copy(s, way, q, sub).wait_send()


def on_device(points, candidates, means, inv_var, log_weight):
    rows, feat = points.shape
    blocks = candidates.shape[0]
    n_dp = lax.axis_size("dp")
    chips = n_dp // 2
    far = chips // 2
    any_space = pl.BlockSpec(memory_space=pl.ANY)
    vmem = pl.BlockSpec(memory_space=pltpu.VMEM)
    sem = pltpu.SemaphoreType.DMA
    wide = 2 * feat
    full = wide + EXTRA
    most = feat + EXTRA
    units = 4 * far
    shapes = (
        jax.ShapeDtypeStruct((2, CB), F32),
        jax.ShapeDtypeStruct((2 * CB, feat), F32),
        jax.ShapeDtypeStruct((2 * CB, feat), F32),
        jax.ShapeDtypeStruct((blocks, RB), F32),
    )
    results = pl.pallas_call(
        functools.partial(kernel, chips),
        out_shape=tuple(pltpu.VMEM(shape.shape, F32) for shape in shapes),
        in_specs=[
            pl.BlockSpec(memory_space=pltpu.SMEM),
            vmem,
            any_space,
            any_space,
            any_space,
        ],
        out_specs=(vmem, vmem, vmem, vmem),
        scratch_shapes=[
            pltpu.VMEM((2 * CB, feat), BF16),
            pltpu.VMEM((2 * CB, feat), BF16),
            pltpu.VMEM((rows, wide), BF16),
            pltpu.VMEM((full, rows), BF16),
            pltpu.VMEM((n_dp, 2, full, CB), BF16),
            pltpu.VMEM((blocks, CANDS, RB, CB), F32),
            pltpu.VMEM((blocks, CANDS + 1, RB, CB), BF16),
            pltpu.VMEM((4, rows, 2 * CB), BF16),
            pltpu.VMEM((max(2 * rows, 4 * most), 2 * CB), F32),
            pltpu.VMEM((4, most, 2 * CB), BF16),
            pltpu.VMEM((units, most, 2 * CB), BF16),
            pltpu.VMEM((2, far, 2, most, 2 * CB), BF16),
            sem((3,)),
            sem((2, far, 2)),
            sem((2, far, 2)),
            sem((chips + 1, 2)),
            sem((chips + 1, 2)),
            sem((units, 3)),
            sem((units, 3)),
            sem((2, far, 2, 3)),
            sem((2, far, 2, 3)),
        ],
        compiler_params=pltpu.CompilerParams(
            collective_id=0, has_side_effects=True, vmem_limit_bytes=60 * 2**20
        ),
        cost_estimate=pl.CostEstimate(
            flops=4 * rows * n_dp * 2 * CB * wide,
            bytes_accessed=(rows + 8 * CB) * feat * 2,
            transcendentals=rows * CANDS * CB,
        ),
    )(candidates.T, log_weight.reshape(2, CB), points, means, inv_var)
    counts, first, second, loglik = results
    return (counts.reshape(-1), first, second, loglik.reshape(-1))


def solution(mesh):
    rows = P(("dp", "comp"))
    wide = P(("dp", "comp"), None)
    return jax.shard_map(
        on_device,
        mesh=mesh,
        in_specs=(wide, wide, wide, wide, rows),
        out_specs=(rows, wide, wide, rows),
        check_vma=False,
    )
```

```python
import functools
import math

import jax
import jax.numpy as jnp
from jax import lax
from jax.experimental import pallas as pl
from jax.experimental.pallas import tpu as pltpu
from jax.sharding import PartitionSpec as P

CB = 128
RB = 128
CANDS = 4
EXTRA = 16
ROW_CHUNK = 1024
MESH = pl.DeviceIdType.MESH
BF16, F32 = jnp.bfloat16, jnp.float32


def kernel(
    chips,
    cand,
    logw,
    points,
    means,
    inv_var,
    counts_out,
    first_out,
    second_out,
    loglik_out,
    mv,
    iv,
    x,
    xt,
    g,
    slots,
    resp,
    wr,
    acc,
    ss,
    sr,
    rr,
    in_sem,
    ag_s,
    ag_r,
    as_s,
    as_r,
    rs_s,
    rs_r,
    rr_s,
    rr_r,
):
    feat = means.shape[1]
    wide = 2 * feat
    blocks = cand.shape[1]
    rows = blocks * RB
    dp = lax.axis_index("dp")
    comp = lax.axis_index("comp")
    owners = lax.axis_size("comp")
    n_dp = 2 * chips
    far = chips // 2
    z, c = dp // 2, lax.rem(dp, 2)
    right = lax.rem(dp + 2, n_dp)
    left = lax.rem(dp + n_dp - 2, n_dp)
    sib = dp + 1 - 2 * c
    ring = (right, left)
    halves = ((0, feat), (feat, feat + EXTRA))

    def share(offset, core):
        return 2 * lax.rem(z + offset + chips, chips) + core

    def remote(src, dst, sems, at, dev):
        return pltpu.make_async_remote_copy(
            src_ref=src,
            dst_ref=dst,
            send_sem=sems[0].at[at],
            recv_sem=sems[1].at[at],
            device_id={"dp": dev},
            device_id_type=MESH,
        )

    load_m = pltpu.make_async_copy(means, mv, in_sem.at[0])
    load_i = pltpu.make_async_copy(inv_var, iv, in_sem.at[1])
    load_p = pltpu.make_async_copy(points, x.at[:, pl.ds(0, feat)], in_sem.at[2])
    load_m.start()
    load_i.start()
    load_p.start()

    barrier = pltpu.get_barrier_semaphore()
    for dev in (left, right, sib):
        pl.semaphore_signal(barrier, inc=1, device_id={"dp": dev}, device_id_type=MESH)

    ring_sems, across = (ag_s, ag_r), (as_s, as_r)

    def start(ref, sems, at, dev):
        remote(ref, ref, sems, at, dev).start()

    def arrive(ref, sems, at):
        remote(ref, ref, sems, at, sib).wait_recv()

    def half(sh, j, p):
        return g.at[sh, j, pl.ds(halves[p][0], halves[p][1])]

    def own_block(j):
        part = pl.ds(j * CB, CB)
        m = mv[part, :].astype(F32)
        v = iv[part, :].astype(F32)
        scaled = v * m
        g[dp, j, pl.ds(0, feat), :] = jnp.transpose(scaled.astype(BF16))
        g[dp, j, pl.ds(feat, feat), :] = jnp.transpose((-0.5 * v).astype(BF16))
        term = jnp.log(v) - scaled * m
        folded = term[:, 0:CB]
        for k in range(1, feat // CB):
            folded = folded + term[:, k * CB : (k + 1) * CB]
        const = 0.5 * jnp.sum(jnp.transpose(folded), axis=0, keepdims=True)
        const = logw[pl.ds(j, 1), :].astype(F32) + const - 0.5 * feat * math.log(2.0 * math.pi)
        high = const.astype(BF16).astype(F32)
        mid = (const - high).astype(BF16).astype(F32)
        low = const - high - mid
        at = lax.broadcasted_iota(jnp.int32, (EXTRA, CB), 0)
        tile = jnp.where(at == 0, high, jnp.where(at == 1, mid, jnp.where(at == 2, low, 0.0)))
        g[dp, j, pl.ds(wide, EXTRA), :] = tile.astype(BF16)
        if j == 0:
            pl.semaphore_wait(barrier, 3)
        start(g.at[dp, j], ring_sems, (0, 0, j), right)
        start(g.at[dp, j], ring_sems, (1, 0, j), left)
        start(g.at[dp, j], across, (0, j), sib)

    load_m.wait()
    load_i.wait()
    own_block(0)
    load_p.wait()

    def spread(i, carry):
        at = pl.ds(pl.multiple_of(i * RB, RB), RB)
        p = x[at, pl.ds(0, feat)]
        pf = p.astype(F32)
        q = (pf * pf).astype(BF16)
        x[at, pl.ds(feat, feat)] = q
        xt[pl.ds(0, feat), at] = jnp.transpose(p)
        xt[pl.ds(feat, feat), at] = jnp.transpose(q)
        xt[pl.ds(wide, EXTRA), at] = jnp.ones((EXTRA, RB), BF16)
        return carry

    lax.fori_loop(0, blocks, spread, 0)
    own_block(1)

    chunk = min(ROW_CHUNK, rows)

    def keep(i, d, bases, consts):
        for r in range(chunk // RB):
            n = i * (chunk // RB) + r
            here = slice(r * RB, (r + 1) * RB)
            low = d[here, 0:CB] + consts[0]
            high = d[here, CB : 2 * CB] + consts[1]
            for s in range(CANDS):
                named = cand[s, n]
                slots[n, s] = jnp.where(
                    named == bases[0], low, jnp.where(named == bases[1], high, slots[n, s])
                )

    def offsets_of(pair):
        bases, consts = [], []
        for sh, j in pair:
            bases.append((sh * owners + comp) * 2 + j)
            tile = g[sh, j, pl.ds(wide, EXTRA), :].astype(F32)
            consts.append(jnp.sum(tile, axis=0, keepdims=True))
        return bases, consts

    def density(pair):
        bases, consts = offsets_of(pair)
        (sh_a, j_a), (sh_b, j_b) = pair

        def body(i, carry):
            at = pl.ds(pl.multiple_of(i * chunk, chunk), chunk)
            cut = pl.ds(0, wide)
            w = jnp.concatenate([g[sh_a, j_a, cut, :], g[sh_b, j_b, cut, :]], axis=1)
            keep(i, jnp.dot(x[at, :], w, preferred_element_type=F32), bases, consts)
            return carry

        lax.fori_loop(0, rows // chunk, body, 0)

    def density_half(sh, p, store):
        cut = pl.ds(pl.multiple_of(p * feat, feat), feat)

        def body(i, carry):
            at = pl.ds(pl.multiple_of(i * chunk, chunk), chunk)
            kept = pl.ds(pl.multiple_of(store * rows + i * chunk, chunk), chunk)
            w = jnp.concatenate([g[sh, 0, cut, :], g[sh, 1, cut, :]], axis=1)
            d = jnp.dot(x[at, cut], w, preferred_element_type=F32)

            @pl.when(p == 0)
            def _():
                acc[kept, :] = d

            @pl.when(p == 1)
            def _():
                keep(i, d + acc[kept, :], *offsets_of(((sh, 0), (sh, 1))))

            return carry

        lax.fori_loop(0, rows // chunk, body, 0)

    def block_of(way, h, e):
        return e if way == 0 else jnp.where(h == 0, e, 1 - e)

    def hop_share(way, h, core):
        return share(-1 - h if way == 0 else 1 + h, core)

    def pair_of(h, e, core):
        return [(hop_share(way, h, core), block_of(way, h, e)) for way in range(2)]

    def receive(h, e):
        for way, (sh, j) in enumerate(pair_of(h, e, c)):
            arrive(g.at[sh, j], ring_sems, (way, h, j))

            @pl.when(h + 1 < far - 1)
            def _(way=way, sh=sh, j=j):
                start(g.at[sh, j], ring_sems, (way, h + 1, j), ring[way])

            @pl.when((h + 1 == far - 1) & (j == way))
            def _(way=way, sh=sh):
                for p in range(2):
                    start(half(sh, way, p), ring_sems, (way, far - 1, p), ring[way])

            start(g.at[sh, j], across, (1 + way * far + h, j), sib)

    def early(t, carry):
        h, e = (t + 1) // 2 - 1, lax.rem(t + 1, 2)

        def one(k, carry):
            core = jnp.where(k == 0, c, 1 - c)
            own = jnp.where(k == 0, dp, sib)
            pair = [
                (jnp.where(t == 0, own, sh), jnp.where(t == 0, way, j))
                for way, (sh, j) in enumerate(pair_of(h, e, core))
            ]

            @pl.when(k == 1)
            def _():
                for way, (sh, j) in enumerate(pair):
                    at = jnp.where(t == 0, 0, 1 + way * far + h)
                    arrive(g.at[sh, j], across, (at, j))

            density(pair)

            @pl.when((k == 0) & (t < 2 * far - 2))
            def _():
                receive(t // 2, lax.rem(t, 2))

            return carry

        lax.fori_loop(0, 2, one, 0)
        return carry

    lax.fori_loop(0, 2 * far - 1, early, 0)

    def late(p, carry):
        sh = share(far, c)
        for part in range(2):

            @pl.when(p == part)
            def _(part=part):
                for way in range(2):
                    arrive(half(sh, way, part), ring_sems, (way, far - 1, part))
                    start(half(sh, way, part), across, (1 + way * far + far - 1, part), sib)

        def one(k, carry):
            target = share(far, jnp.where(k == 0, c, 1 - c))
            for part in range(2):

                @pl.when((k == 1) & (p == part))
                def _(part=part):
                    for way in range(2):
                        at = (1 + way * far + far - 1, part)
                        arrive(half(target, way, part), across, at)

            density_half(target, p, k)
            return carry

        lax.fori_loop(0, 2, one, 0)
        return carry

    lax.fori_loop(0, 2, late, 0)

    def soften(n):
        d = [slots[n, s] for s in range(CANDS)]
        peak = jnp.max(
            jnp.maximum(jnp.maximum(d[0], d[1]), jnp.maximum(d[2], d[3])), axis=1, keepdims=True
        )
        e = [jnp.exp(v - peak) for v in d]
        total = jnp.sum((e[0] + e[1]) + (e[2] + e[3]), axis=1, keepdims=True)
        scale = 1.0 / total
        for s in range(CANDS):
            resp[n, s] = (e[s] * scale).astype(BF16)
        resp[n, CANDS] = jnp.zeros((RB, CB), BF16)
        slots[n, 0] = jnp.broadcast_to(peak + jnp.log(total), (RB, CB))

    def soften_some(i, carry):
        for k in range(4):
            soften(4 * i + k)
        return carry

    lax.fori_loop(0, blocks // 4, soften_some, 0)

    def sent():
        for way in range(2):
            for h in range(far):
                for p in range(2):
                    ref = g.at[0, 0] if h < far - 1 else half(0, 0, p)
                    remote(ref, ref, ring_sems, (way, h, p), sib).wait_send()
                    remote(ref, ref, across, (1 + way * far + h, p), sib).wait_send()
        for j in range(2):
            remote(g.at[0, 0], g.at[0, 0], across, (0, j), sib).wait_send()

    room = acc.shape[0] // 4
    sum_sems, pair_sems = (rr_s, rr_r), (rs_s, rs_r)
    part = feat // 2

    def fill(k, lv):
        way, core = k // 2, jnp.where(lax.rem(k, 2) == 0, 1 - c, c)
        sh = share(jnp.where(way == 0, far - lv, lv - far), core)
        base = (sh * owners + comp) * 2

        def body(n, carry):
            for j in range(2):
                pick = jnp.int32(CANDS)
                for s in range(CANDS):
                    pick = jnp.where(cand[s, n] == base + j, s, pick)
                here = pl.ds(pl.multiple_of(n * RB, RB), RB)
                wr[k, here, pl.ds(j * CB, CB)] = resp[n, pick]
            return carry

        lax.fori_loop(0, blocks, body, 0)

    def place(sub):
        return pl.ds(pl.multiple_of(sub * part, part), part) if sub is not None else pl.ds(feat, EXTRA)

    def ss_copy(s, way, q, sub):
        at = (2 * s + way, 2 if sub is None else sub)
        return remote(
            ss.at[2 * way + q, place(sub)], sr.at[2 * s + way, place(sub)], pair_sems, at, sib
        )

    def rr_copy(s, way, q, sub):
        lv = (s + 1) // 2
        at = (way, lv, q, 2 if sub is None else sub)
        return remote(
            sr.at[2 * s + way, place(sub)], rr.at[way, lv, q, place(sub)], sum_sems, at, ring[way]
        )

    def on_way(way, act):
        for w in range(2):

            @pl.when(way == w)
            def _(w=w):
                act(w)

    def step(s, carry):
        lv, e = (s + 1) // 2, lax.rem(s + 1, 2)
        shared = (lv == 0) | (lv == far)

        @pl.when((s == 0) | (e == 0))
        def _():
            def body(k, carry):
                fill(k, lv)
                return carry

            lax.fori_loop(0, jnp.where(shared, 2, 4), body, 0)

        def one(k, carry):
            core, sub, way = lax.rem(k // 2, 2), k // 4, lax.rem(k, 2)
            q = jnp.where(e == 1, way, 1 - way)
            slot = 2 * way + q

            def product(low, size):
                return jnp.dot(
                    xt[pl.ds(low, size), :], wr[jnp.where(shared, core, 2 * way + core)], preferred_element_type=F32
                )

            def put(value, where):
                @pl.when(core == 0)
                def _():
                    @pl.when(s >= 2)
                    def _():
                        ss_copy(s - 2, way, q, where).wait_send()

                    ss[slot, place(where), :] = value.astype(BF16)
                    ss_copy(s, way, q, where).start()

                @pl.when(core == 1)
                def _():
                    start = sub * part if where is not None else feat
                    acc[pl.ds(pl.multiple_of(slot * room + start, 16), value.shape[0]), :] = value

            put(product(pl.multiple_of(q * feat + sub * part, part), part), sub)

            @pl.when((q == 1) & (sub == 1))
            def _():
                put(product(wide, EXTRA), None)

            def combine(where, tile, count):
                ss_copy(s, way, q, where).wait_recv()
                level = lv - 1

                def add(extra):
                    def body(r, carry):
                        start = (sub * part if where is not None else feat) + r * tile
                        start = pl.multiple_of(start, 16)
                        here = pl.ds(start, tile)
                        t = acc[pl.ds(pl.multiple_of(slot * room + start, 16), tile), :]
                        t = t + sr[2 * s + way, here, :].astype(F32)
                        if extra:
                            t = t + rr[way, level, q, here, :].astype(F32)
                        sr[2 * s + way, here, :] = t.astype(BF16)
                        return carry

                    lax.fori_loop(0, count, body, 0)

                @pl.when(s < 2)
                def _():
                    add(False)

                @pl.when((s >= 2) & (lv < far))
                def _():
                    before = jnp.where(s == 2, 0, s - 2)
                    on_way(way, lambda w: rr_copy(before, w, q, where).wait_recv())
                    add(True)

                @pl.when(lv < far)
                def _():
                    on_way(way, lambda w: rr_copy(s, w, q, where).start())

            @pl.when(core == 1)
            def _():
                count = max(k for k in range(1, 9) if part // 16 % k == 0)
                combine(sub, 16 * count, part // (16 * count))

                @pl.when((q == 1) & (sub == 1))
                def _():
                    combine(None, EXTRA, 1)

            return carry

        lax.fori_loop(0, 8, one, 0)

        @pl.when(s == 1)
        def _():
            def out(n, carry):
                norm = jnp.transpose(slots[n, 0])[0:1, :]
                loglik_out[pl.ds(n, 1), :] = norm / feat
                return carry

            lax.fori_loop(0, blocks, out, 0)

        return carry

    lax.fori_loop(0, 2 * far, step, 0)

    last = 2 * far - 1

    def final_of(q, start, size):
        way = 1 - q
        t = acc[pl.ds((2 * way + q) * room + start, size), :]
        t = t + sr[2 * last + way, pl.ds(start, size), :].astype(F32)
        for w in range(2):
            t = t + rr[w, far - 1, q, pl.ds(start, size), :].astype(F32)
        return t

    def done(q, sub):
        for w in range(2):
            rr_copy(last - 1 if q == w else last - 2, w, q, sub).wait_recv()

    for sub in range(2):
        for q in range(2):
            done(q, sub)
            out = second_out if q else first_out
            edges = list(range(sub * part, (sub + 1) * part, min(CB, part)))
            for low in edges:
                t = final_of(q, low, min(CB, part))
                out[:, pl.ds(low, min(CB, part))] = jnp.transpose(t)
    done(1, None)
    t = final_of(1, feat, EXTRA)
    for j in range(2):
        counts_out[pl.ds(j, 1), :] = t[0:1, j * CB : (j + 1) * CB]

    sent()
    for s in range(2 * far):
        for way in range(2):
            q = way if s % 2 == 0 else 1 - way
            for sub in (0, 1) if q == 0 else (0, 1, None):
                if s >= last - 1:
                    ss_copy(s, way, q, sub).wait_send()
                if s < last:
                    rr_copy(s, way, q, sub).wait_send()


def copy_out(*refs):
    sources, targets, sems = refs[:4], refs[4:8], refs[8]
    copies = [
        pltpu.make_async_copy(s, t, sems.at[i]) for i, (s, t) in enumerate(zip(sources, targets))
    ]
    for copy in copies:
        copy.start()
    for copy in copies:
        copy.wait()


def on_device(points, candidates, means, inv_var, log_weight):
    rows, feat = points.shape
    blocks = candidates.shape[0]
    n_dp = lax.axis_size("dp")
    chips = n_dp // 2
    far = chips // 2
    any_space = pl.BlockSpec(memory_space=pl.ANY)
    vmem = pl.BlockSpec(memory_space=pltpu.VMEM)
    sem = pltpu.SemaphoreType.DMA
    wide = 2 * feat
    full = wide + EXTRA
    most = feat + EXTRA
    units = 4 * far
    shapes = (
        jax.ShapeDtypeStruct((2, CB), F32),
        jax.ShapeDtypeStruct((2 * CB, feat), F32),
        jax.ShapeDtypeStruct((2 * CB, feat), F32),
        jax.ShapeDtypeStruct((blocks, RB), F32),
    )
    results = pl.pallas_call(
        functools.partial(kernel, chips),
        out_shape=tuple(pltpu.VMEM(shape.shape, F32) for shape in shapes),
        in_specs=[
            pl.BlockSpec(memory_space=pltpu.SMEM),
            vmem,
            any_space,
            any_space,
            any_space,
        ],
        out_specs=(vmem, vmem, vmem, vmem),
        scratch_shapes=[
            pltpu.VMEM((2 * CB, feat), BF16),
            pltpu.VMEM((2 * CB, feat), BF16),
            pltpu.VMEM((rows, wide), BF16),
            pltpu.VMEM((full, rows), BF16),
            pltpu.VMEM((n_dp, 2, full, CB), BF16),
            pltpu.VMEM((blocks, CANDS, RB, CB), F32),
            pltpu.VMEM((blocks, CANDS + 1, RB, CB), BF16),
            pltpu.VMEM((4, rows, 2 * CB), BF16),
            pltpu.VMEM((max(2 * rows, 4 * most), 2 * CB), F32),
            pltpu.VMEM((4, most, 2 * CB), BF16),
            pltpu.VMEM((units, most, 2 * CB), BF16),
            pltpu.VMEM((2, far, 2, most, 2 * CB), BF16),
            sem((3,)),
            sem((2, far, 2)),
            sem((2, far, 2)),
            sem((chips + 1, 2)),
            sem((chips + 1, 2)),
            sem((units, 3)),
            sem((units, 3)),
            sem((2, far, 2, 3)),
            sem((2, far, 2, 3)),
        ],
        compiler_params=pltpu.CompilerParams(
            collective_id=0, has_side_effects=True, vmem_limit_bytes=60 * 2**20
        ),
        cost_estimate=pl.CostEstimate(
            flops=4 * rows * n_dp * 2 * CB * wide,
            bytes_accessed=(rows + 8 * CB) * feat * 2,
            transcendentals=rows * CANDS * CB,
        ),
    )(candidates.T, log_weight.reshape(2, CB), points, means, inv_var)
    held = [pltpu.with_memory_space_constraint(r, pltpu.VMEM) for r in results]
    counts, first, second, loglik = pl.pallas_call(
        copy_out,
        out_shape=shapes,
        in_specs=[any_space] * 4,
        out_specs=(any_space,) * 4,
        scratch_shapes=[sem((4,))],
    )(*held)
    return (counts.reshape(-1), first, second, loglik.reshape(-1))


def solution(mesh):
    rows = P(("dp", "comp"))
    wide = P(("dp", "comp"), None)
    return jax.shard_map(
        on_device,
        mesh=mesh,
        in_specs=(wide, wide, wide, wide, rows),
        out_specs=(rows, wide, wide, rows),
        check_vma=False,
    )
```

```python
import functools
import math

import jax
import jax.numpy as jnp
from jax import lax
from jax.experimental import pallas as pl
from jax.experimental.pallas import tpu as pltpu
from jax.sharding import PartitionSpec as P

CB = 128
RB = 128
CANDS = 4
EXTRA = 16
ROW_CHUNK = 1024
MESH = pl.DeviceIdType.MESH
BF16, F32 = jnp.bfloat16, jnp.float32


def kernel(
    chips,
    cand,
    logw,
    points,
    means,
    inv_var,
    counts_out,
    first_out,
    second_out,
    loglik_out,
    mv,
    iv,
    x,
    xt,
    g,
    slots,
    resp,
    wr,
    acc,
    ss,
    sr,
    rr,
    in_sem,
    ag_s,
    ag_r,
    as_s,
    as_r,
    rs_s,
    rs_r,
    rr_s,
    rr_r,
):
    feat = means.shape[1]
    wide = 2 * feat
    blocks = cand.shape[1]
    rows = blocks * RB
    dp = lax.axis_index("dp")
    comp = lax.axis_index("comp")
    owners = lax.axis_size("comp")
    n_dp = 2 * chips
    far = chips // 2
    z, c = dp // 2, lax.rem(dp, 2)
    right = lax.rem(dp + 2, n_dp)
    left = lax.rem(dp + n_dp - 2, n_dp)
    sib = dp + 1 - 2 * c
    ring = (right, left)
    halves = ((0, feat), (feat, feat + EXTRA))

    def share(offset, core):
        return 2 * lax.rem(z + offset + chips, chips) + core

    def remote(src, dst, sems, at, dev):
        return pltpu.make_async_remote_copy(
            src_ref=src,
            dst_ref=dst,
            send_sem=sems[0].at[at],
            recv_sem=sems[1].at[at],
            device_id={"dp": dev},
            device_id_type=MESH,
        )

    load_m = pltpu.make_async_copy(means, mv, in_sem.at[0])
    load_i = pltpu.make_async_copy(inv_var, iv, in_sem.at[1])
    load_p = pltpu.make_async_copy(points, x.at[:, pl.ds(0, feat)], in_sem.at[2])
    load_m.start()
    load_i.start()
    load_p.start()

    barrier = pltpu.get_barrier_semaphore()
    for dev in (left, right, sib):
        pl.semaphore_signal(barrier, inc=1, device_id={"dp": dev}, device_id_type=MESH)

    ring_sems, across = (ag_s, ag_r), (as_s, as_r)

    def start(ref, sems, at, dev):
        remote(ref, ref, sems, at, dev).start()

    def arrive(ref, sems, at):
        remote(ref, ref, sems, at, sib).wait_recv()

    def half(sh, j, p):
        return g.at[sh, j, pl.ds(halves[p][0], halves[p][1])]

    def own_block(j):
        part = pl.ds(j * CB, CB)
        m = mv[part, :].astype(F32)
        v = iv[part, :].astype(F32)
        scaled = v * m
        g[dp, j, pl.ds(0, feat), :] = jnp.transpose(scaled.astype(BF16))
        g[dp, j, pl.ds(feat, feat), :] = jnp.transpose((-0.5 * v).astype(BF16))
        term = jnp.log(v) - scaled * m
        folded = term[:, 0:CB]
        for k in range(1, feat // CB):
            folded = folded + term[:, k * CB : (k + 1) * CB]
        const = 0.5 * jnp.sum(jnp.transpose(folded), axis=0, keepdims=True)
        const = logw[pl.ds(j, 1), :].astype(F32) + const - 0.5 * feat * math.log(2.0 * math.pi)
        high = const.astype(BF16).astype(F32)
        mid = (const - high).astype(BF16).astype(F32)
        low = const - high - mid
        at = lax.broadcasted_iota(jnp.int32, (EXTRA, CB), 0)
        tile = jnp.where(at == 0, high, jnp.where(at == 1, mid, jnp.where(at == 2, low, 0.0)))
        g[dp, j, pl.ds(wide, EXTRA), :] = tile.astype(BF16)
        if j == 0:
            pl.semaphore_wait(barrier, 3)
        start(g.at[dp, j], ring_sems, (0, 0, j), right)
        start(g.at[dp, j], ring_sems, (1, 0, j), left)
        start(g.at[dp, j], across, (0, j), sib)

    load_m.wait()
    load_i.wait()
    own_block(0)
    load_p.wait()

    def spread(i, carry):
        at = pl.ds(pl.multiple_of(i * RB, RB), RB)
        p = x[at, pl.ds(0, feat)]
        pf = p.astype(F32)
        q = (pf * pf).astype(BF16)
        x[at, pl.ds(feat, feat)] = q
        xt[pl.ds(0, feat), at] = jnp.transpose(p)
        xt[pl.ds(feat, feat), at] = jnp.transpose(q)
        xt[pl.ds(wide, EXTRA), at] = jnp.ones((EXTRA, RB), BF16)
        return carry

    lax.fori_loop(0, blocks, spread, 0)
    own_block(1)

    chunk = min(ROW_CHUNK, rows)

    def keep(i, d, bases, consts):
        for r in range(chunk // RB):
            n = i * (chunk // RB) + r
            here = slice(r * RB, (r + 1) * RB)
            low = d[here, 0:CB] + consts[0]
            high = d[here, CB : 2 * CB] + consts[1]
            for s in range(CANDS):
                named = cand[s, n]
                slots[n, s] = jnp.where(
                    named == bases[0], low, jnp.where(named == bases[1], high, slots[n, s])
                )

    def offsets_of(pair):
        bases, consts = [], []
        for sh, j in pair:
            bases.append((sh * owners + comp) * 2 + j)
            tile = g[sh, j, pl.ds(wide, EXTRA), :].astype(F32)
            consts.append(jnp.sum(tile, axis=0, keepdims=True))
        return bases, consts

    def density(pair):
        bases, consts = offsets_of(pair)
        (sh_a, j_a), (sh_b, j_b) = pair

        def body(i, carry):
            at = pl.ds(pl.multiple_of(i * chunk, chunk), chunk)
            cut = pl.ds(0, wide)
            w = jnp.concatenate([g[sh_a, j_a, cut, :], g[sh_b, j_b, cut, :]], axis=1)
            keep(i, jnp.dot(x[at, :], w, preferred_element_type=F32), bases, consts)
            return carry

        lax.fori_loop(0, rows // chunk, body, 0)

    def density_half(sh, p, store):
        cut = pl.ds(pl.multiple_of(p * feat, feat), feat)

        def body(i, carry):
            at = pl.ds(pl.multiple_of(i * chunk, chunk), chunk)
            kept = pl.ds(pl.multiple_of(store * rows + i * chunk, chunk), chunk)
            w = jnp.concatenate([g[sh, 0, cut, :], g[sh, 1, cut, :]], axis=1)
            d = jnp.dot(x[at, cut], w, preferred_element_type=F32)

            @pl.when(p == 0)
            def _():
                acc[kept, :] = d

            @pl.when(p == 1)
            def _():
                keep(i, d + acc[kept, :], *offsets_of(((sh, 0), (sh, 1))))

            return carry

        lax.fori_loop(0, rows // chunk, body, 0)

    def block_of(way, h, e):
        return e if way == 0 else jnp.where(h == 0, e, 1 - e)

    def hop_share(way, h, core):
        return share(-1 - h if way == 0 else 1 + h, core)

    def pair_of(h, e, core):
        return [(hop_share(way, h, core), block_of(way, h, e)) for way in range(2)]

    def receive(h, e):
        for way, (sh, j) in enumerate(pair_of(h, e, c)):
            arrive(g.at[sh, j], ring_sems, (way, h, j))

            @pl.when(h + 1 < far - 1)
            def _(way=way, sh=sh, j=j):
                start(g.at[sh, j], ring_sems, (way, h + 1, j), ring[way])

            @pl.when((h + 1 == far - 1) & (j == way))
            def _(way=way, sh=sh):
                for p in range(2):
                    start(half(sh, way, p), ring_sems, (way, far - 1, p), ring[way])

            start(g.at[sh, j], across, (1 + way * far + h, j), sib)

    def early(t, carry):
        h, e = (t + 1) // 2 - 1, lax.rem(t + 1, 2)

        def one(k, carry):
            core = jnp.where(k == 0, c, 1 - c)
            own = jnp.where(k == 0, dp, sib)
            pair = [
                (jnp.where(t == 0, own, sh), jnp.where(t == 0, way, j))
                for way, (sh, j) in enumerate(pair_of(h, e, core))
            ]

            @pl.when(k == 1)
            def _():
                for way, (sh, j) in enumerate(pair):
                    at = jnp.where(t == 0, 0, 1 + way * far + h)
                    arrive(g.at[sh, j], across, (at, j))

            density(pair)

            @pl.when((k == 0) & (t < 2 * far - 2))
            def _():
                receive(t // 2, lax.rem(t, 2))

            return carry

        lax.fori_loop(0, 2, one, 0)
        return carry

    lax.fori_loop(0, 2 * far - 1, early, 0)

    def late(p, carry):
        sh = share(far, c)
        for part in range(2):

            @pl.when(p == part)
            def _(part=part):
                for way in range(2):
                    arrive(half(sh, way, part), ring_sems, (way, far - 1, part))
                    start(half(sh, way, part), across, (1 + way * far + far - 1, part), sib)

        def one(k, carry):
            target = share(far, jnp.where(k == 0, c, 1 - c))
            for part in range(2):

                @pl.when((k == 1) & (p == part))
                def _(part=part):
                    for way in range(2):
                        at = (1 + way * far + far - 1, part)
                        arrive(half(target, way, part), across, at)

            density_half(target, p, k)
            return carry

        lax.fori_loop(0, 2, one, 0)
        return carry

    lax.fori_loop(0, 2, late, 0)

    def soften(n):
        d = [slots[n, s] for s in range(CANDS)]
        peak = jnp.max(
            jnp.maximum(jnp.maximum(d[0], d[1]), jnp.maximum(d[2], d[3])), axis=1, keepdims=True
        )
        e = [jnp.exp(v - peak) for v in d]
        total = jnp.sum((e[0] + e[1]) + (e[2] + e[3]), axis=1, keepdims=True)
        scale = 1.0 / total
        for s in range(CANDS):
            resp[n, s] = (e[s] * scale).astype(BF16)
        resp[n, CANDS] = jnp.zeros((RB, CB), BF16)
        slots[n, 0] = jnp.broadcast_to(peak + jnp.log(total), (RB, CB))

    def soften_some(i, carry):
        for k in range(4):
            soften(4 * i + k)
        return carry

    lax.fori_loop(0, blocks // 4, soften_some, 0)

    def sent():
        for way in range(2):
            for h in range(far):
                for p in range(2):
                    ref = g.at[0, 0] if h < far - 1 else half(0, 0, p)
                    remote(ref, ref, ring_sems, (way, h, p), sib).wait_send()
                    remote(ref, ref, across, (1 + way * far + h, p), sib).wait_send()
        for j in range(2):
            remote(g.at[0, 0], g.at[0, 0], across, (0, j), sib).wait_send()

    room = acc.shape[0] // 4
    sum_sems, pair_sems = (rr_s, rr_r), (rs_s, rs_r)
    part = feat // 3

    def fill(k, lv):
        way, core = k // 2, jnp.where(lax.rem(k, 2) == 0, 1 - c, c)
        sh = share(jnp.where(way == 0, far - lv, lv - far), core)
        base = (sh * owners + comp) * 2

        def body(n, carry):
            for j in range(2):
                pick = jnp.int32(CANDS)
                for s in range(CANDS):
                    pick = jnp.where(cand[s, n] == base + j, s, pick)
                here = pl.ds(pl.multiple_of(n * RB, RB), RB)
                wr[k, here, pl.ds(j * CB, CB)] = resp[n, pick]
            return carry

        lax.fori_loop(0, blocks, body, 0)

    def place(sub):
        return pl.ds(pl.multiple_of(sub * part, part), part) if sub is not None else pl.ds(feat, EXTRA)

    def ss_copy(s, way, q, sub):
        at = (2 * s + way, 3 if sub is None else sub)
        return remote(
            ss.at[2 * way + q, place(sub)], sr.at[2 * s + way, place(sub)], pair_sems, at, sib
        )

    def rr_copy(s, way, q, sub):
        lv = (s + 1) // 2
        at = (way, lv, q, 3 if sub is None else sub)
        return remote(
            sr.at[2 * s + way, place(sub)], rr.at[way, lv, q, place(sub)], sum_sems, at, ring[way]
        )

    def on_way(way, act):
        for w in range(2):

            @pl.when(way == w)
            def _(w=w):
                act(w)

    def step(s, carry):
        lv, e = (s + 1) // 2, lax.rem(s + 1, 2)
        shared = (lv == 0) | (lv == far)

        @pl.when((s == 0) | (e == 0))
        def _():
            def body(k, carry):
                fill(k, lv)
                return carry

            lax.fori_loop(0, jnp.where(shared, 2, 4), body, 0)

        def one(k, carry):
            core, sub, way = lax.rem(k // 2, 2), k // 4, lax.rem(k, 2)
            q = jnp.where(e == 1, way, 1 - way)
            slot = 2 * way + q

            def product(low, size):
                return jnp.dot(
                    xt[pl.ds(low, size), :], wr[jnp.where(shared, core, 2 * way + core)], preferred_element_type=F32
                )

            def put(value, where):
                @pl.when(core == 0)
                def _():
                    @pl.when(s >= 2)
                    def _():
                        ss_copy(s - 2, way, q, where).wait_send()

                    ss[slot, place(where), :] = value.astype(BF16)
                    ss_copy(s, way, q, where).start()

                @pl.when(core == 1)
                def _():
                    start = sub * part if where is not None else feat
                    acc[pl.ds(pl.multiple_of(slot * room + start, 16), value.shape[0]), :] = value

            put(product(pl.multiple_of(q * feat + sub * part, part), part), sub)

            @pl.when((q == 1) & (sub == 2))
            def _():
                put(product(wide, EXTRA), None)

            def combine(where, tile, count):
                ss_copy(s, way, q, where).wait_recv()
                level = lv - 1

                def add(extra):
                    def body(r, carry):
                        start = (sub * part if where is not None else feat) + r * tile
                        start = pl.multiple_of(start, 16)
                        here = pl.ds(start, tile)
                        t = acc[pl.ds(pl.multiple_of(slot * room + start, 16), tile), :]
                        t = t + sr[2 * s + way, here, :].astype(F32)
                        if extra:
                            t = t + rr[way, level, q, here, :].astype(F32)
                        sr[2 * s + way, here, :] = t.astype(BF16)
                        return carry

                    lax.fori_loop(0, count, body, 0)

                @pl.when(s < 2)
                def _():
                    add(False)

                @pl.when((s >= 2) & (lv < far))
                def _():
                    before = jnp.where(s == 2, 0, s - 2)
                    on_way(way, lambda w: rr_copy(before, w, q, where).wait_recv())
                    add(True)

                @pl.when(lv < far)
                def _():
                    on_way(way, lambda w: rr_copy(s, w, q, where).start())

            @pl.when(core == 1)
            def _():
                count = max(k for k in range(1, 9) if part // 16 % k == 0)
                combine(sub, 16 * count, part // (16 * count))

                @pl.when((q == 1) & (sub == 2))
                def _():
                    combine(None, EXTRA, 1)

            return carry

        lax.fori_loop(0, 12, one, 0)

        @pl.when(s == 1)
        def _():
            def out(n, carry):
                norm = jnp.transpose(slots[n, 0])[0:1, :]
                loglik_out[pl.ds(n, 1), :] = norm / feat
                return carry

            lax.fori_loop(0, blocks, out, 0)

        return carry

    lax.fori_loop(0, 2 * far, step, 0)

    last = 2 * far - 1

    def final_of(q, start, size):
        way = 1 - q
        t = acc[pl.ds((2 * way + q) * room + start, size), :]
        t = t + sr[2 * last + way, pl.ds(start, size), :].astype(F32)
        for w in range(2):
            t = t + rr[w, far - 1, q, pl.ds(start, size), :].astype(F32)
        return t

    def done(q, sub):
        for w in range(2):
            rr_copy(last - 1 if q == w else last - 2, w, q, sub).wait_recv()

    for sub in range(3):
        for q in range(2):
            done(q, sub)
            out = second_out if q else first_out
            edges = list(range(sub * part, (sub + 1) * part, min(CB, part)))
            for low in edges:
                t = final_of(q, low, min(CB, part))
                out[:, pl.ds(low, min(CB, part))] = jnp.transpose(t)
    done(1, None)
    t = final_of(1, feat, EXTRA)
    for j in range(2):
        counts_out[pl.ds(j, 1), :] = t[0:1, j * CB : (j + 1) * CB]

    sent()
    for s in range(2 * far):
        for way in range(2):
            q = way if s % 2 == 0 else 1 - way
            for sub in (0, 1, 2) if q == 0 else (0, 1, 2, None):
                if s >= last - 1:
                    ss_copy(s, way, q, sub).wait_send()
                if s < last:
                    rr_copy(s, way, q, sub).wait_send()


def copy_out(*refs):
    sources, targets, sems = refs[:4], refs[4:8], refs[8]
    copies = [
        pltpu.make_async_copy(s, t, sems.at[i]) for i, (s, t) in enumerate(zip(sources, targets))
    ]
    for copy in copies:
        copy.start()
    for copy in copies:
        copy.wait()


def on_device(points, candidates, means, inv_var, log_weight):
    rows, feat = points.shape
    blocks = candidates.shape[0]
    n_dp = lax.axis_size("dp")
    chips = n_dp // 2
    far = chips // 2
    any_space = pl.BlockSpec(memory_space=pl.ANY)
    vmem = pl.BlockSpec(memory_space=pltpu.VMEM)
    sem = pltpu.SemaphoreType.DMA
    wide = 2 * feat
    full = wide + EXTRA
    most = feat + EXTRA
    units = 4 * far
    shapes = (
        jax.ShapeDtypeStruct((2, CB), F32),
        jax.ShapeDtypeStruct((2 * CB, feat), F32),
        jax.ShapeDtypeStruct((2 * CB, feat), F32),
        jax.ShapeDtypeStruct((blocks, RB), F32),
    )
    results = pl.pallas_call(
        functools.partial(kernel, chips),
        out_shape=tuple(pltpu.VMEM(shape.shape, F32) for shape in shapes),
        in_specs=[
            pl.BlockSpec(memory_space=pltpu.SMEM),
            vmem,
            any_space,
            any_space,
            any_space,
        ],
        out_specs=(vmem, vmem, vmem, vmem),
        scratch_shapes=[
            pltpu.VMEM((2 * CB, feat), BF16),
            pltpu.VMEM((2 * CB, feat), BF16),
            pltpu.VMEM((rows, wide), BF16),
            pltpu.VMEM((full, rows), BF16),
            pltpu.VMEM((n_dp, 2, full, CB), BF16),
            pltpu.VMEM((blocks, CANDS, RB, CB), F32),
            pltpu.VMEM((blocks, CANDS + 1, RB, CB), BF16),
            pltpu.VMEM((4, rows, 2 * CB), BF16),
            pltpu.VMEM((max(2 * rows, 4 * most), 2 * CB), F32),
            pltpu.VMEM((4, most, 2 * CB), BF16),
            pltpu.VMEM((units, most, 2 * CB), BF16),
            pltpu.VMEM((2, far, 2, most, 2 * CB), BF16),
            sem((3,)),
            sem((2, far, 2)),
            sem((2, far, 2)),
            sem((chips + 1, 2)),
            sem((chips + 1, 2)),
            sem((units, 4)),
            sem((units, 4)),
            sem((2, far, 2, 4)),
            sem((2, far, 2, 4)),
        ],
        compiler_params=pltpu.CompilerParams(
            collective_id=0, has_side_effects=True, vmem_limit_bytes=60 * 2**20
        ),
        cost_estimate=pl.CostEstimate(
            flops=4 * rows * n_dp * 2 * CB * wide,
            bytes_accessed=(rows + 8 * CB) * feat * 2,
            transcendentals=rows * CANDS * CB,
        ),
    )(candidates.T, log_weight.reshape(2, CB), points, means, inv_var)
    held = [pltpu.with_memory_space_constraint(r, pltpu.VMEM) for r in results]
    counts, first, second, loglik = pl.pallas_call(
        copy_out,
        out_shape=shapes,
        in_specs=[any_space] * 4,
        out_specs=(any_space,) * 4,
        scratch_shapes=[sem((4,))],
    )(*held)
    return (counts.reshape(-1), first, second, loglik.reshape(-1))


def solution(mesh):
    rows = P(("dp", "comp"))
    wide = P(("dp", "comp"), None)
    return jax.shard_map(
        on_device,
        mesh=mesh,
        in_specs=(wide, wide, wide, wide, rows),
        out_specs=(rows, wide, wide, rows),
        check_vma=False,
    )
```
